256 devices in a mesh: dp: 4 (over x), expert: 64 (over y, z, core).
Axes of the slice: x: 4, y: 4, z: 8, core: 2. Of those that a mesh axis runs over, the one named last changes fastest.
Arguments:
- tokens: bfloat16 [32768, 4096], P(('dp', 'expert')), may hold values from -6 to 6
- expert_ids: int32 [32768, 2], P(('dp', 'expert')), may hold values from 0 to 63, all different within a row; in each aligned block of 128 rows (0 to 127, 128 to 255, ...) at most 5 rows name the same one
- gate_values: bfloat16 [32768, 2], P(('dp', 'expert')), may hold values from 0.19921875 to 1
- pair_order: int32 [256, 128], P(('dp', 'expert')), may hold values from 0 to 127, each once within a row
- w_gate: bfloat16 [64, 4096, 1536], P('expert', None, 'dp'), may hold values from -0.09375 to 0.09375
- w_up: bfloat16 [64, 4096, 1536], P('expert', None, 'dp'), may hold values from -0.09375 to 0.09375
- w_down: bfloat16 [64, 1536, 4096], P('expert', 'dp'), may hold values from -0.15625 to 0.15625
- sketch: bfloat16 [4096, 256], P('expert'), may hold values from -0.09375 to 0.09375
Outputs:
- mixed: bfloat16 [32768, 4096], P(('dp', 'expert'))
- reading: float32 [4096, 256], P(('dp', 'expert'))
The draws below stay inside these ranges and needn't reach their ends.
Inputs may be any that keep to these rules, and one draw needn't show every extreme that they name: `expert_ids`: each row names 2 different experts; among the rows of one device no expert is named more than 5 times, a bound that some block reaches. `pair_order`: each row is a permutation of 0 .. 127, given as row numbers inside its device's block; entries 2 p and 2 p + 1 are the positive and the negative token of pair p.
All inputs are finite; a program needn't handle non-finite values.
Results may differ from the reference program's by a relative error of at most 0.022.
Values may be sent and summed in bfloat16 or wider, within the bound.
No kernel may reach another device: no remote copies, remote signals or barrier semaphores. Data moves between devices by JAX's collectives and lax.ppermute only.
A program may use at most 128 MiB of HBM per device.

```python
import math
import jax
import jax.numpy as jnp
import numpy as np
from jax import lax

D = 4096
FF = 1536
TOPK = 2
SKETCH = 256
TOK_DEV = 128
EXPERTS = 64
CAPS = 5
TOKENS = 32768
PAIRS = 16384
N_DP = 4
DEVICES = 256


def levels(own_key, extent, shards, least, high):
    factor_of = 1.0
    for position, blocks in shards:
        heights = jax.random.uniform(jax.random.fold_in(jax.random.fold_in(own_key, 6), position), (blocks,), jnp.float32, least / len(shards), high / len(shards))
        factor_of = factor_of * jnp.repeat(jnp.exp(heights), extent[position] // blocks).reshape((-1,) + (1,) * (len(extent) - 1 - position))
    return factor_of


def assign_block(rng, own, number, rows, number_of, top, limit, skew):
    order = jax.random.permutation(rng, number_of)
    crowded, ordinary = portions_of(number_of, rows * top, limit, skew, True), portions_of(number_of, rows * top, limit, skew, False)
    places = jnp.arange(number_of)

    def named(tallies, rotation):
        used = int((tallies > 0).sum())
        fixed = max(1, used // 4)
        shifted = fixed + (places - fixed + rotation * (used - fixed)) % max(1, number_of - fixed)
        return jnp.zeros((number_of,), jnp.int32).at[order[jnp.where(places < fixed, places, shifted)]].set(jnp.asarray(tallies, jnp.int32))

    tallies = jnp.where(number % 4 == 0, named(crowded, number // 4), named(ordinary, number - number // 4 - 1))
    mixed = jax.random.permutation(jax.random.fold_in(own, 3), number_of)
    source_of, receiver = mixed[0:number_of // 2 * 2:2], mixed[1:number_of // 2 * 2:2]
    slack = jnp.minimum(tallies[source_of] - 1, limit - tallies[receiver]) // 2
    slack = jnp.where((source_of == order[0]) | (receiver == order[0]) | (tallies[receiver] == 0), 0, jnp.maximum(slack, 0))
    shifted = jax.random.randint(jax.random.fold_in(own, 4), (number_of // 2,), 0, 1 << 20) % (slack + 1)
    tallies = tallies.at[source_of].add(-shifted).at[receiver].add(shifted)
    labels = jnp.searchsorted(jnp.cumsum(tallies), jnp.arange(rows * top), side="right").astype(jnp.int32)
    listing = labels.reshape(top, rows).T
    listing = listing[jax.random.permutation(jax.random.fold_in(own, 1), rows)]
    rotation = jax.random.randint(jax.random.fold_in(own, 2), (rows, 1), 0, top)
    return jnp.take_along_axis(listing, (jnp.arange(top)[None, :] + rotation) % top, axis=1)


def portions_of(amount, total, reach, lean, full):
    weights = [(1 << 20) // math.isqrt(rank ** lean) + 1 for rank in range(1, amount + 1)]
    largest = reach if full else min(reach, max(-(-total // amount), total * weights[0] // sum(weights)))
    least = 1 if total - largest >= amount - 1 else 0
    given, rest = [largest] + [least] * (amount - 1), total - largest - least * (amount - 1)
    while rest > 0:
        free = [i for i in range(1, amount) if given[i] < largest] or [i for i in range(1, amount) if given[i] < reach]
        mass, left = sum([weights[i] for i in free]), rest
        for i in free:
            addition = min(reach - given[i], max(1, left * weights[i] // mass), rest)
            given[i] = given[i] + addition
            rest = rest - addition
    return np.array(given)


def bell_draw(key, extent, scale, most, cuts=(), kind=jnp.bfloat16):
    result = scale * jax.random.normal(key, extent, jnp.float32)
    if cuts:
        result = result * levels(key, extent, cuts, -0.22, 0.18)
    return jnp.clip(result, -most, most).astype(kind)


def setup_inputs(seed: int = 0) -> dict:
    key_list = jax.random.split(jax.random.key(seed), 9)
    tokens = bell_draw(key_list[0], (TOKENS, D), 1.0, 6.0, ((0, 256),))
    expert_ids_keys = jax.random.split(jax.random.fold_in(key_list[1], 1), TOKENS // TOK_DEV)
    expert_ids_turns = jax.random.permutation(jax.random.fold_in(key_list[1], 3), TOKENS // TOK_DEV)
    expert_ids = jax.vmap(lambda own, number: assign_block(jax.random.fold_in(key_list[1], 2), own, number, TOK_DEV, EXPERTS, TOPK, CAPS, 2))(expert_ids_keys, expert_ids_turns).reshape((TOKENS, TOPK))
    gate_values = jnp.clip(0.19921875 + 0.80078125 * jax.random.uniform(key_list[2], (TOKENS, TOPK), jnp.float32) ** levels(key_list[2], (TOKENS, TOPK), ((0, 256),), -0.2, 0.2), 0.19921875, 1.0).astype(jnp.bfloat16)
    pair_order = jax.vmap(lambda own: jax.random.permutation(own, TOK_DEV))(jax.random.split(key_list[3], DEVICES)).reshape((DEVICES, TOK_DEV)).astype(jnp.int32)
    w_gate = bell_draw(key_list[4], (EXPERTS, D, FF), D ** -0.5, 0.09375, ((0, 64), (2, 4)))
    w_up = bell_draw(key_list[5], (EXPERTS, D, FF), D ** -0.5, 0.09375, ((0, 64), (2, 4)))
    w_down = bell_draw(key_list[6], (EXPERTS, FF, D), FF ** -0.5, 0.15625, ((0, 64), (1, 4)))
    sketch = bell_draw(key_list[7], (D, SKETCH), D ** -0.5, 0.09375, ((0, 64),))
    return dict(tokens=tokens, expert_ids=expert_ids, gate_values=gate_values, pair_order=pair_order, w_gate=w_gate, w_up=w_up, w_down=w_down, sketch=sketch)


def reference(tokens, expert_ids, gate_values, pair_order, w_gate, w_up, w_down, sketch):
    device_count = TOKENS // TOK_DEV
    flat_ids = expert_ids.reshape(device_count, TOK_DEV * TOPK)
    onehot = (flat_ids[:, :, None] == jnp.arange(EXPERTS, dtype=jnp.int32)[None, None, :]).astype(jnp.int32)
    slot_rank = lax.optimization_barrier(jnp.sum((jnp.cumsum(onehot, axis=1) - onehot) * onehot, axis=2)).astype(jnp.int32)
    block_index = jnp.arange(device_count, dtype=jnp.int32)[:, None]
    column = (block_index * CAPS + slot_rank).astype(jnp.int32)
    token_index = (block_index * TOK_DEV + (jnp.arange(TOK_DEV * TOPK, dtype=jnp.int32) // TOPK)[None, :]).astype(jnp.int32)
    source = jnp.full((EXPERTS, device_count * CAPS), -1, jnp.int32)
    source = source.at[flat_ids.reshape(-1), column.reshape(-1)].set(token_index.reshape(-1))
    hidden = FF // N_DP

    def expert_out(packed):
        row_index, gate_proj, up_proj, down_proj = packed
        picked = tokens[jnp.maximum(row_index, 0)]
        picked = jnp.where(row_index[:, None] >= 0, picked, jnp.zeros((), jnp.bfloat16))
        gate_act = jnp.dot(picked, gate_proj, preferred_element_type=jnp.float32)
        up_act = jnp.dot(picked, up_proj, preferred_element_type=jnp.float32)
        activation = (jax.nn.silu(gate_act) * up_act).astype(jnp.bfloat16)
        running = jnp.zeros((picked.shape[0], D), jnp.float32)
        for hidden_part in range(N_DP):
            partial_out = jnp.dot(activation[:, hidden_part * hidden:(hidden_part + 1) * hidden], down_proj[hidden_part * hidden:(hidden_part + 1) * hidden], preferred_element_type=jnp.float32).astype(jnp.bfloat16)
            partial_out = lax.optimization_barrier(partial_out)
            running = running + partial_out.astype(jnp.float32)
        return running.astype(jnp.bfloat16)
    outputs = lax.map(expert_out, (source, w_gate, w_up, w_down))
    token_column = column.reshape(TOKENS, TOPK)
    mixed_sum = jnp.zeros((TOKENS, D), jnp.float32)
    for chosen in range(TOPK):
        rows_k = outputs[expert_ids[:, chosen], token_column[:, chosen]]
        mixed_sum = mixed_sum + gate_values[:, chosen].astype(jnp.float32)[:, None] * rows_k.astype(jnp.float32)
    mixed = mixed_sum.astype(jnp.bfloat16)
    offsets = jnp.arange(device_count, dtype=jnp.int32)[:, None] * TOK_DEV
    positive = (offsets + pair_order[:, 0::2]).reshape(-1).astype(jnp.int32)
    negative = (offsets + pair_order[:, 1::2]).reshape(-1).astype(jnp.int32)
    contrast = (mixed[positive].astype(jnp.float32) - mixed[negative].astype(jnp.float32)).astype(jnp.bfloat16)
    projected = jnp.dot(contrast, sketch, preferred_element_type=jnp.float32).astype(jnp.bfloat16)
    covariance = lax.dot_general(contrast, projected, (((0,), (0,)), ((), ())), preferred_element_type=jnp.float32)
    reading = covariance * (1.0 / math.sqrt(PAIRS))
    return (mixed, reading)
```

```python
import math

import jax
import jax.numpy as jnp
from jax import lax
from jax.sharding import PartitionSpec as P

CHUNKS = (1, 2, 2)


def pick_ranks(ids):
    rows = ids.shape[0]
    earlier = jnp.arange(rows)[None, :] < jnp.arange(rows)[:, None]
    same = ids[:, :, None, None] == ids[None, None, :, :]
    return jnp.sum((same & earlier[:, None, :, None]).astype(jnp.int32), axis=(2, 3))


def shards(tokens, expert_ids, gate_values, pair_order, w_gate, w_up, w_down, sketch):
    rows_dev, width = tokens.shape
    experts = lax.axis_size("expert")
    groups = lax.axis_size("dp")
    lanes = 128
    tall = width // lanes
    gate_proj, up_proj, down_proj = w_gate[0], w_up[0], w_down[0]
    ranks = pick_ranks(expert_ids)

    def place_of(first, count):
        inside = (ranks >= first) & (ranks < first + count)
        return jnp.where(inside, expert_ids * count + ranks - first, -1)

    places, first = [], 0
    for count in CHUNKS:
        places.append(place_of(first, count))
        first += count

    full_sketch = lax.all_gather(sketch, "expert", axis=0, tiled=True)

    arrived = []
    for count, place in zip(CHUNKS, places):
        spots = jnp.arange(experts * count, dtype=jnp.int32)
        select = jnp.any(place[None, :, :] == spots[:, None, None], axis=2)
        placed = jnp.dot(select.astype(jnp.bfloat16), tokens, preferred_element_type=jnp.float32)
        outgoing = placed.astype(jnp.bfloat16).reshape(experts, count * tall, lanes)
        incoming = lax.all_to_all(outgoing, "expert", split_axis=0, concat_axis=0, tiled=True)
        arrived.append(incoming.reshape(experts * count, width))

    mixed_sum = jnp.zeros((rows_dev, width), jnp.float32)
    for count, place, rows in zip(CHUNKS, places, arrived):
        picked = lax.all_gather(rows, "dp", axis=0, tiled=True)
        gate_act = jnp.dot(picked, gate_proj, preferred_element_type=jnp.float32)
        up_act = jnp.dot(picked, up_proj, preferred_element_type=jnp.float32)
        activation = (jax.nn.silu(gate_act) * up_act).astype(jnp.bfloat16)
        partial = jnp.dot(activation, down_proj, preferred_element_type=jnp.float32)
        summed = lax.psum_scatter(
            partial.astype(jnp.bfloat16), "dp", scatter_dimension=0, tiled=True
        )
        summed = summed.reshape(experts, count * tall, lanes)
        returned = lax.all_to_all(summed, "expert", split_axis=0, concat_axis=0, tiled=True)
        returned = returned.reshape(experts * count, width)
        spots = jnp.arange(experts * count, dtype=jnp.int32)
        matches = place[:, :, None] == spots[None, None, :]
        weights = jnp.sum(
            jnp.where(matches, gate_values[:, :, None], jnp.zeros((), jnp.bfloat16)), axis=1
        )
        mixed_sum = mixed_sum + jnp.dot(weights, returned, preferred_element_type=jnp.float32)
    mixed = mixed_sum.astype(jnp.bfloat16)

    pairs = rows_dev // 2
    order = pair_order[0].reshape(pairs, 2)
    row_ids = jnp.arange(rows_dev, dtype=jnp.int32)
    signs = (order[:, 0:1] == row_ids[None, :]).astype(jnp.bfloat16) - (
        order[:, 1:2] == row_ids[None, :]
    ).astype(jnp.bfloat16)
    contrast = jnp.dot(signs, mixed, preferred_element_type=jnp.float32).astype(jnp.bfloat16)
    projected = jnp.dot(contrast, full_sketch, preferred_element_type=jnp.float32)
    projected = lax.all_gather(projected.astype(jnp.bfloat16), "dp", axis=0, tiled=True)
    columns = jnp.transpose(contrast.reshape(pairs, groups, width // groups), (1, 0, 2))
    columns = lax.all_to_all(columns, "dp", split_axis=0, concat_axis=0, tiled=True)
    columns = columns.reshape(groups * pairs, width // groups)
    covariance = lax.dot_general(
        columns, projected, (((0,), (0,)), ((), ())), preferred_element_type=jnp.float32
    )
    parts = covariance.astype(jnp.bfloat16).reshape(experts, -1, covariance.shape[1])
    parts = lax.all_to_all(parts, "expert", split_axis=0, concat_axis=0, tiled=True)
    reading = jnp.sum(parts.astype(jnp.float32), axis=0)
    reading = reading * (1.0 / math.sqrt(pairs * groups * experts))
    return (mixed, reading)


def solution(mesh):
    return jax.shard_map(
        shards,
        mesh=mesh,
        in_specs=(
            P(("dp", "expert"), None),
            P(("dp", "expert"), None),
            P(("dp", "expert"), None),
            P(("dp", "expert"), None),
            P("expert", None, "dp"),
            P("expert", None, "dp"),
            P("expert", "dp", None),
            P("expert", None),
        ),
        out_specs=(P(("dp", "expert"), None), P(("dp", "expert"), None)),
        check_vma=False,
    )
```

```python
import math

import jax
import jax.numpy as jnp
from jax import lax
from jax.experimental import pallas as pl
from jax.experimental.pallas import tpu as pltpu
from jax.sharding import PartitionSpec as P

CHUNKS = (3, 2)
VMEM = 58 * 2**20


def shift(x, by):
    size = lax.axis_size("dp")
    return lax.ppermute(x, "dp", [(i, (i + by) % size) for i in range(size)])


def pick_ranks(ids):
    rows = ids.shape[0]
    earlier = jnp.arange(rows)[None, :] < jnp.arange(rows)[:, None]
    same = ids[:, :, None, None] == ids[None, None, :, :]
    return jnp.sum((same & earlier[:, None, :, None]).astype(jnp.int32), axis=(2, 3))


def gather_neighbours(own):
    top, end = own
    left_top, right_end = shift(top, 1), shift(end, -1)
    left_end, right_top = shift(end, 1), shift(top, -1)
    return left_top, left_end, right_top, right_end


def hidden_kernel(steps, place_ref, *refs):
    rows, (gate_ref, up_ref, out_ref, gate_sum, up_sum) = refs[:8], refs[8:]
    size = 2 * rows[0].shape[0]
    step = pl.program_id(0)

    @pl.when(step == 0)
    def _():
        gate_sum[...] = jnp.zeros_like(gate_sum)
        up_sum[...] = jnp.zeros_like(up_sum)

    x = jnp.concatenate([r[...] for r in rows], axis=0)
    gate_sum[...] += jnp.dot(x, gate_ref[0], preferred_element_type=jnp.float32)
    up_sum[...] += jnp.dot(x, up_ref[0], preferred_element_type=jnp.float32)

    @pl.when(step == steps - 1)
    def _():
        for i, by in enumerate((0, 3, 1, 2)):
            part = pl.ds(i * size, size)
            gate = gate_sum[part, :]
            act = gate / (1.0 + jnp.exp(-gate)) * up_sum[part, :]
            start = pl.multiple_of(lax.rem(place_ref[0] + by, 4) * size, size)
            out_ref[pl.ds(start, size), :] = act.astype(out_ref.dtype)


def hidden_units(rows, w_gate, w_up):
    half, width = rows[0].shape
    hidden = w_gate.shape[2]
    block = 1024
    steps = width // block
    total = 8 * half
    place = lax.axis_index("dp").astype(jnp.int32).reshape(1)
    return pl.pallas_call(
        lambda *refs: hidden_kernel(steps, *refs),
        grid_spec=pltpu.PrefetchScalarGridSpec(
            num_scalar_prefetch=1,
            grid=(steps,),
            in_specs=[pl.BlockSpec((half, block), lambda i, p: (0, i))] * 8
            + [pl.BlockSpec((1, block, hidden), lambda i, p: (0, i, 0))] * 2,
            out_specs=pl.BlockSpec((total, hidden), lambda i, p: (0, 0)),
            scratch_shapes=[pltpu.VMEM((total, hidden), jnp.float32)] * 2,
        ),
        out_shape=jax.ShapeDtypeStruct((total, hidden), jnp.bfloat16),
        compiler_params=pltpu.CompilerParams(vmem_limit_bytes=VMEM),
        cost_estimate=pl.CostEstimate(
            flops=4 * total * width * hidden,
            bytes_accessed=2 * (2 * width * hidden + total * width),
            transcendentals=total * hidden,
        ),
    )(place, *rows, w_gate, w_up)


def down_kernel(*refs):
    acts, downs, out_ref = refs[:4], refs[4:8], refs[8]
    out = jnp.dot(acts[0][...], downs[0][...], preferred_element_type=jnp.float32)
    for act, down in zip(acts[1:], downs[1:]):
        out += jnp.dot(act[...], down[...], preferred_element_type=jnp.float32)
    out_ref[...] = out.astype(out_ref.dtype)


def down_product(acts, downs):
    rows, hidden = acts[0].shape
    width = downs[0].shape[1]
    block = 256
    return pl.pallas_call(
        down_kernel,
        grid=(width // block,),
        in_specs=[pl.BlockSpec((rows, hidden), lambda i: (0, 0))] * 4
        + [pl.BlockSpec((hidden, block), lambda i: (0, i))] * 4,
        out_specs=pl.BlockSpec((rows, block), lambda i: (0, i)),
        out_shape=jax.ShapeDtypeStruct((rows, width), jnp.bfloat16),
        compiler_params=pltpu.CompilerParams(vmem_limit_bytes=VMEM),
        cost_estimate=pl.CostEstimate(
            flops=8 * rows * hidden * width,
            bytes_accessed=2 * (4 * hidden * width + rows * width + 4 * rows * hidden),
            transcendentals=0,
        ),
    )(*acts, *downs)


def shards(tokens, expert_ids, gate_values, pair_order, w_gate, w_up, w_down, sketch):
    rows_dev, width = tokens.shape
    experts = lax.axis_size("expert")
    groups = lax.axis_size("dp")
    lanes = 128
    tall = width // lanes
    ranks = pick_ranks(expert_ids)

    def place_of(first, count):
        inside = (ranks >= first) & (ranks < first + count)
        return jnp.where(inside, expert_ids * count + ranks - first, -1)

    places, first = [], 0
    for count in CHUNKS:
        places.append(place_of(first, count))
        first += count

    place = lax.axis_index("dp")
    columns = width // groups

    def down_columns(by):
        start = lax.rem(place + by, groups) * columns
        return lax.dynamic_slice_in_dim(w_down[0], start, columns, axis=1)

    down_parts = tuple(down_columns(by) for by in (0, 1, groups - 1, 2))
    full_sketch = lax.all_gather(sketch, "expert", axis=0, tiled=True)

    arrived = []
    for i, (count, place) in enumerate(zip(CHUNKS, places)):
        spots = jnp.arange(experts * count, dtype=jnp.int32)
        select = jnp.any(place[None, :, :] == spots[:, None, None], axis=2)
        placed = jnp.dot(select.astype(jnp.bfloat16), tokens, preferred_element_type=jnp.float32)
        outgoing = placed.astype(jnp.bfloat16).reshape(experts, count * tall, lanes)
        if i == 0:
            outgoing, down_parts = lax.optimization_barrier((outgoing, down_parts))
            downs = tuple(shift(part, by) if by else part for part, by in zip(down_parts, (0, 1, -1, 2)))
        elif i == 1:
            outgoing, downs = lax.optimization_barrier((outgoing, downs))
        incoming = lax.all_to_all(outgoing, "expert", split_axis=0, concat_axis=0, tiled=True)
        arrived.append(incoming)

    middle = experts // 2
    last = len(CHUNKS) - 1
    owns, firsts, seconds = [], [], []
    for i, count in enumerate(CHUNKS):
        parts = (arrived[i][:middle], arrived[i][middle:])
        own = tuple(part.reshape(middle * count, width) for part in parts)
        first = gather_neighbours(own)
        if i < last:
            first, arrived[i + 1] = lax.optimization_barrier((first, arrived[i + 1]))
        owns.append(own)
        firsts.append(first)
        seconds.append((shift(first[0], 1), shift(first[3], -1)))

    acts, outs = [], []

    done = full_sketch
    for i in range(len(CHUNKS)):
        second = seconds[i]
        if i < last:
            second, firsts[i + 1], done = lax.optimization_barrier((second, firsts[i + 1], done))
            seconds[i + 1] = (shift(firsts[i + 1][0], 1), shift(firsts[i + 1][3], -1))
        else:
            second, done = lax.optimization_barrier((second, done))
        if i == 0:
            full_sketch = done
        elif i > 1:
            outs[i - 2] = done
        act = hidden_units((*owns[i], *firsts[i], *second), w_gate, w_up)
        sent = (act, shift(act, 1), shift(act, -1), shift(act, 2))
        acts.append(sent)
        if i:
            acts[i - 1], act = lax.optimization_barrier((acts[i - 1], act))
            acts[i] = (act, *acts[i][1:])
            outs.append(down_product(acts[i - 1], downs))
            done = outs[i - 1]
        else:
            done = ()
    acts[last], outs[last - 1] = lax.optimization_barrier((acts[last], outs[last - 1]))
    outs.append(down_product(acts[last], downs))

    mixed_sum = jnp.zeros((groups, rows_dev, columns), jnp.float32)
    back = ()
    for count, place, out in zip(CHUNKS, places, outs):
        out = out.reshape(groups * experts, count * (columns // lanes), lanes)
        out, back = lax.optimization_barrier((out, back))
        back = lax.all_to_all(out, ("dp", "expert"), split_axis=0, concat_axis=0, tiled=True)
        back = back.reshape(groups, experts * count, columns)
        spots = jnp.arange(experts * count, dtype=jnp.int32)
        matches = place[:, :, None] == spots[None, None, :]
        weights = jnp.sum(
            jnp.where(matches, gate_values[:, :, None], jnp.zeros((), jnp.bfloat16)), axis=1
        )
        mixed_sum = mixed_sum + jnp.einsum(
            "ts,gsc->gtc", weights, back, preferred_element_type=jnp.float32
        )
    mixed_parts = mixed_sum.astype(jnp.bfloat16)
    mixed = jnp.transpose(mixed_parts, (1, 0, 2)).reshape(rows_dev, width)

    pairs = rows_dev // 2
    order = pair_order[0].reshape(pairs, 2)
    row_ids = jnp.arange(rows_dev, dtype=jnp.int32)
    signs = (order[:, 0:1] == row_ids[None, :]).astype(jnp.bfloat16) - (
        order[:, 1:2] == row_ids[None, :]
    ).astype(jnp.bfloat16)
    contrast = jnp.einsum("pt,gtc->gpc", signs, mixed_parts, preferred_element_type=jnp.float32)
    contrast = contrast.astype(jnp.bfloat16)
    sent = lax.all_to_all(contrast, "dp", split_axis=0, concat_axis=0, tiled=True)
    projected = jnp.einsum(
        "gpc,gck->pk",
        contrast,
        full_sketch.reshape(groups, columns, -1),
        preferred_element_type=jnp.float32,
    ).astype(jnp.bfloat16)
    nearby = (projected, shift(projected, -1), shift(projected, 2), shift(projected, 1))
    here = lax.axis_index("dp")
    projected = jnp.concatenate(
        [
            lax.select_n(lax.rem(g - here + groups, groups), *nearby)
            for g in range(groups)
        ],
        axis=0,
    )
    covariance = lax.dot_general(
        sent.reshape(groups * pairs, columns),
        projected,
        (((0,), (0,)), ((), ())),
        preferred_element_type=jnp.float32,
    )
    parts = covariance.astype(jnp.bfloat16).reshape(experts, -1, covariance.shape[1])
    parts = lax.all_to_all(parts, "expert", split_axis=0, concat_axis=0, tiled=True)
    reading = jnp.sum(parts.astype(jnp.float32), axis=0)
    reading = reading * (1.0 / math.sqrt(pairs * groups * experts))
    return (mixed, reading)


def solution(mesh):
    return jax.shard_map(
        shards,
        mesh=mesh,
        in_specs=(
            P(("dp", "expert"), None),
            P(("dp", "expert"), None),
            P(("dp", "expert"), None),
            P(("dp", "expert"), None),
            P("expert", None, "dp"),
            P("expert", None, "dp"),
            P("expert", "dp", None),
            P("expert", None),
        ),
        out_specs=(P(("dp", "expert"), None), P(("dp", "expert"), None)),
        check_vma=False,
    )
```

```python
import math

import jax
import jax.numpy as jnp
from jax import lax
from jax.experimental import pallas as pl
from jax.experimental.pallas import tpu as pltpu
from jax.sharding import PartitionSpec as P

CHUNKS = (3, 2)
VMEM = 58 * 2**20


def shift(x, by):
    size = lax.axis_size("dp")
    return lax.ppermute(x, "dp", [(i, (i + by) % size) for i in range(size)])


def pick_ranks(ids):
    rows = ids.shape[0]
    earlier = jnp.arange(rows)[None, :] < jnp.arange(rows)[:, None]
    same = ids[:, :, None, None] == ids[None, None, :, :]
    return jnp.sum((same & earlier[:, None, :, None]).astype(jnp.int32), axis=(2, 3))


def gather_neighbours(own):
    top, end = own
    left_top, right_end = shift(top, 1), shift(end, -1)
    left_end, right_top = shift(end, 1), shift(top, -1)
    return left_top, left_end, right_top, right_end


def hidden_kernel(steps, place_ref, *refs):
    rows, (gate_ref, up_ref, out_ref, gate_sum, up_sum) = refs[:8], refs[8:]
    size = 2 * rows[0].shape[0]
    step = pl.program_id(0)

    @pl.when(step == 0)
    def _():
        gate_sum[...] = jnp.zeros_like(gate_sum)
        up_sum[...] = jnp.zeros_like(up_sum)

    x = jnp.concatenate([r[...] for r in rows], axis=0)
    gate_sum[...] += jnp.dot(x, gate_ref[0], preferred_element_type=jnp.float32)
    up_sum[...] += jnp.dot(x, up_ref[0], preferred_element_type=jnp.float32)

    @pl.when(step == steps - 1)
    def _():
        for i, by in enumerate((0, 3, 1, 2)):
            part = pl.ds(i * size, size)
            gate = gate_sum[part, :]
            act = gate / (1.0 + jnp.exp(-gate)) * up_sum[part, :]
            start = pl.multiple_of(lax.rem(place_ref[0] + by, 4) * size, size)
            out_ref[pl.ds(start, size), :] = act.astype(out_ref.dtype)


def hidden_units(rows, w_gate, w_up):
    half, width = rows[0].shape
    hidden = w_gate.shape[2]
    block = 1024
    steps = width // block
    total = 8 * half
    place = lax.axis_index("dp").astype(jnp.int32).reshape(1)
    return pl.pallas_call(
        lambda *refs: hidden_kernel(steps, *refs),
        grid_spec=pltpu.PrefetchScalarGridSpec(
            num_scalar_prefetch=1,
            grid=(steps,),
            in_specs=[pl.BlockSpec((half, block), lambda i, p: (0, i))] * 8
            + [pl.BlockSpec((1, block, hidden), lambda i, p: (0, i, 0))] * 2,
            out_specs=pl.BlockSpec((total, hidden), lambda i, p: (0, 0)),
            scratch_shapes=[pltpu.VMEM((total, hidden), jnp.float32)] * 2,
        ),
        out_shape=jax.ShapeDtypeStruct((total, hidden), jnp.bfloat16),
        compiler_params=pltpu.CompilerParams(vmem_limit_bytes=VMEM),
        cost_estimate=pl.CostEstimate(
            flops=4 * total * width * hidden,
            bytes_accessed=2 * (2 * width * hidden + total * width),
            transcendentals=total * hidden,
        ),
    )(place, *rows, w_gate, w_up)


def down_kernel(*refs):
    acts, downs, out_ref = refs[:4], refs[4:8], refs[8]
    out = jnp.dot(acts[0][...], downs[0][...], preferred_element_type=jnp.float32)
    for act, down in zip(acts[1:], downs[1:]):
        out += jnp.dot(act[...], down[...], preferred_element_type=jnp.float32)
    out_ref[...] = out.reshape(out_ref.shape).astype(out_ref.dtype)


def down_product(acts, downs):
    rows, hidden = acts[0].shape
    width = downs[0].shape[1]
    block = 256
    tall = width // 128
    return pl.pallas_call(
        down_kernel,
        grid=(rows // block,),
        in_specs=[pl.BlockSpec((block, hidden), lambda i: (i, 0))] * 4
        + [pl.BlockSpec((hidden, width), lambda i: (0, 0))] * 4,
        out_specs=pl.BlockSpec((block, tall, 128), lambda i: (i, 0, 0)),
        out_shape=jax.ShapeDtypeStruct((rows, tall, 128), jnp.bfloat16),
        compiler_params=pltpu.CompilerParams(vmem_limit_bytes=VMEM),
        cost_estimate=pl.CostEstimate(
            flops=8 * rows * hidden * width,
            bytes_accessed=2 * (4 * hidden * width + rows * width + 4 * rows * hidden),
            transcendentals=0,
        ),
    )(*acts, *downs)


def shards(tokens, expert_ids, gate_values, pair_order, w_gate, w_up, w_down, sketch):
    rows_dev, width = tokens.shape
    experts = lax.axis_size("expert")
    groups = lax.axis_size("dp")
    lanes = 128
    tall = width // lanes
    ranks = pick_ranks(expert_ids)

    def place_of(first, count):
        inside = (ranks >= first) & (ranks < first + count)
        return jnp.where(inside, expert_ids * count + ranks - first, -1)

    places, first = [], 0
    for count in CHUNKS:
        places.append(place_of(first, count))
        first += count

    place = lax.axis_index("dp")
    columns = width // groups

    def down_columns(by):
        start = lax.rem(place + by, groups) * columns
        return lax.dynamic_slice_in_dim(w_down[0], start, columns, axis=1)

    down_parts = tuple(down_columns(by) for by in (0, 1, groups - 1, 2))
    def outgoing_rows(count, place):
        spots = jnp.arange(experts * count, dtype=jnp.int32)
        select = jnp.any(place[None, :, :] == spots[:, None, None], axis=2)
        placed = jnp.dot(select.astype(jnp.bfloat16), tokens, preferred_element_type=jnp.float32)
        return placed.astype(jnp.bfloat16).reshape(experts, count * tall, lanes)

    def halves(incoming, count):
        middle = experts // 2
        parts = (incoming[:middle], incoming[middle:])
        return tuple(part.reshape(middle * count, width) for part in parts)

    def dispatch(outgoing):
        return lax.all_to_all(outgoing, "expert", split_axis=0, concat_axis=0, tiled=True)

    outgoing, down_parts = lax.optimization_barrier(
        (outgoing_rows(CHUNKS[0], places[0]), down_parts)
    )
    downs = tuple(shift(part, by) if by else part for part, by in zip(down_parts, (0, 1, -1, 2)))
    own = halves(dispatch(outgoing), CHUNKS[0])
    next_outgoing = outgoing_rows(CHUNKS[1], places[1])
    next_outgoing, own = lax.optimization_barrier((next_outgoing, own))
    next_outgoing, downs = lax.optimization_barrier((next_outgoing, downs))
    next_arrived = dispatch(next_outgoing)
    first = gather_neighbours(own)
    next_arrived, _, _ = lax.optimization_barrier((next_arrived, first[0], first[3]))
    second = (shift(first[0], 1), shift(first[3], -1))
    late_sketch, next_arrived = lax.optimization_barrier((sketch, next_arrived))
    full_sketch = lax.all_gather(late_sketch, "expert", axis=0, tiled=True)
    next_own = halves(next_arrived, CHUNKS[1])
    next_first = list(gather_neighbours(next_own))
    second, _, _ = lax.optimization_barrier(
        (second, next_first[0], next_first[3])
    )
    next_second = (shift(next_first[0], 1), shift(next_first[3], -1))
    act = hidden_units((*own, *first, *second), w_gate, w_up)
    acts = (act, shift(act, 1), shift(act, -1), shift(act, 2))
    next_second, act = lax.optimization_barrier((next_second, act))
    next_act = hidden_units((*next_own, *next_first, *next_second), w_gate, w_up)
    next_acts = (next_act, shift(next_act, 1), shift(next_act, -1), shift(next_act, 2))
    acts, next_act = lax.optimization_barrier((acts, next_act))
    next_acts = (next_act, *next_acts[1:])
    out = down_product(acts, downs)
    next_acts, _ = lax.optimization_barrier((next_acts, out))
    next_acts, full_sketch = lax.optimization_barrier((next_acts, full_sketch))
    outs = (out, down_product(next_acts, downs))

    mixed_sum = jnp.zeros((groups, rows_dev, columns), jnp.float32)
    back = ()
    for count, place, out in zip(CHUNKS, places, outs):
        out = out.reshape(groups * experts, count * (columns // lanes), lanes)
        out, back = lax.optimization_barrier((out, back))
        back = lax.all_to_all(out, ("dp", "expert"), split_axis=0, concat_axis=0, tiled=True)
        back = back.reshape(groups, experts * count, columns)
        spots = jnp.arange(experts * count, dtype=jnp.int32)
        matches = place[:, :, None] == spots[None, None, :]
        weights = jnp.sum(
            jnp.where(matches, gate_values[:, :, None], jnp.zeros((), jnp.bfloat16)), axis=1
        )
        mixed_sum = mixed_sum + jnp.einsum(
            "ts,gsc->gtc", weights, back, preferred_element_type=jnp.float32
        )
    mixed_parts = mixed_sum.astype(jnp.bfloat16)
    mixed = jnp.transpose(mixed_parts, (1, 0, 2)).reshape(rows_dev, width)

    pairs = rows_dev // 2
    order = pair_order[0].reshape(pairs, 2)
    row_ids = jnp.arange(rows_dev, dtype=jnp.int32)
    signs = (order[:, 0:1] == row_ids[None, :]).astype(jnp.bfloat16) - (
        order[:, 1:2] == row_ids[None, :]
    ).astype(jnp.bfloat16)
    contrast = jnp.einsum("pt,gtc->gpc", signs, mixed_parts, preferred_element_type=jnp.float32)
    contrast = contrast.astype(jnp.bfloat16)
    sent = lax.all_to_all(contrast, "dp", split_axis=0, concat_axis=0, tiled=True)
    projected = jnp.einsum(
        "gpc,gck->pk",
        contrast,
        full_sketch.reshape(groups, columns, -1),
        preferred_element_type=jnp.float32,
    ).astype(jnp.bfloat16)
    nearby = (projected, shift(projected, -1), shift(projected, 2), shift(projected, 1))
    here = lax.axis_index("dp")
    projected = jnp.concatenate(
        [
            lax.select_n(lax.rem(g - here + groups, groups), *nearby)
            for g in range(groups)
        ],
        axis=0,
    )
    covariance = lax.dot_general(
        sent.reshape(groups * pairs, columns),
        projected,
        (((0,), (0,)), ((), ())),
        preferred_element_type=jnp.float32,
    )
    parts = covariance.astype(jnp.bfloat16).reshape(experts, -1, covariance.shape[1])
    parts = lax.all_to_all(parts, "expert", split_axis=0, concat_axis=0, tiled=True)
    reading = jnp.sum(parts.astype(jnp.float32), axis=0)
    reading = reading * (1.0 / math.sqrt(pairs * groups * experts))
    return (mixed, reading)


def solution(mesh):
    return jax.shard_map(
        shards,
        mesh=mesh,
        in_specs=(
            P(("dp", "expert"), None),
            P(("dp", "expert"), None),
            P(("dp", "expert"), None),
            P(("dp", "expert"), None),
            P("expert", None, "dp"),
            P("expert", None, "dp"),
            P("expert", "dp", None),
            P("expert", None),
        ),
        out_specs=(P(("dp", "expert"), None), P(("dp", "expert"), None)),
        check_vma=False,
    )
```

```python
import math

import jax
import jax.numpy as jnp
from jax import lax
from jax.experimental import pallas as pl
from jax.experimental.pallas import tpu as pltpu
from jax.sharding import PartitionSpec as P

CHUNKS = (3, 2)
VMEM = 58 * 2**20


def shift(x, by):
    size = lax.axis_size("dp")
    return lax.ppermute(x, "dp", [(i, (i + by) % size) for i in range(size)])


def pick_ranks(ids):
    rows = ids.shape[0]
    earlier = jnp.arange(rows)[None, :] < jnp.arange(rows)[:, None]
    same = ids[:, :, None, None] == ids[None, None, :, :]
    return jnp.sum((same & earlier[:, None, :, None]).astype(jnp.int32), axis=(2, 3))


def gather_neighbours(own):
    top, end = own
    left_top, right_end = shift(top, 1), shift(end, -1)
    left_end, right_top = shift(end, 1), shift(top, -1)
    return left_top, left_end, right_top, right_end


def hidden_kernel(steps, place_ref, *refs):
    rows, (gate_ref, up_ref, out_ref, gate_sum, up_sum) = refs[:8], refs[8:]
    size = 2 * rows[0].shape[0]
    step = pl.program_id(0)

    @pl.when(step == 0)
    def _():
        gate_sum[...] = jnp.zeros_like(gate_sum)
        up_sum[...] = jnp.zeros_like(up_sum)

    x = jnp.concatenate([r[...] for r in rows], axis=0)
    gate_sum[...] += jnp.dot(x, gate_ref[0], preferred_element_type=jnp.float32)
    up_sum[...] += jnp.dot(x, up_ref[0], preferred_element_type=jnp.float32)

    @pl.when(step == steps - 1)
    def _():
        for i, by in enumerate((0, 3, 1, 2)):
            part = pl.ds(i * size, size)
            gate = gate_sum[part, :]
            act = gate / (1.0 + jnp.exp(-gate)) * up_sum[part, :]
            start = pl.multiple_of(lax.rem(place_ref[0] + by, 4) * size, size)
            out_ref[pl.ds(start, size), :] = act.astype(out_ref.dtype)


def hidden_units(rows, w_gate, w_up):
    half, width = rows[0].shape
    hidden = w_gate.shape[2]
    block = 1024
    steps = width // block
    total = 8 * half
    place = lax.axis_index("dp").astype(jnp.int32).reshape(1)
    return pl.pallas_call(
        lambda *refs: hidden_kernel(steps, *refs),
        grid_spec=pltpu.PrefetchScalarGridSpec(
            num_scalar_prefetch=1,
            grid=(steps,),
            in_specs=[pl.BlockSpec((half, block), lambda i, p: (0, i))] * 8
            + [pl.BlockSpec((1, block, hidden), lambda i, p: (0, i, 0))] * 2,
            out_specs=pl.BlockSpec((total, hidden), lambda i, p: (0, 0)),
            scratch_shapes=[pltpu.VMEM((total, hidden), jnp.float32)] * 2,
        ),
        out_shape=jax.ShapeDtypeStruct((total, hidden), jnp.bfloat16),
        compiler_params=pltpu.CompilerParams(vmem_limit_bytes=VMEM),
        cost_estimate=pl.CostEstimate(
            flops=4 * total * width * hidden,
            bytes_accessed=2 * (2 * width * hidden + total * width),
            transcendentals=total * hidden,
        ),
    )(place, *rows, w_gate, w_up)


def down_kernel(*refs):
    acts, downs, out_ref = refs[:4], refs[4:8], refs[8]
    out = jnp.dot(acts[0][...], downs[0][...], preferred_element_type=jnp.float32)
    for act, down in zip(acts[1:], downs[1:]):
        out += jnp.dot(act[...], down[...], preferred_element_type=jnp.float32)
    out_ref[...] = out.reshape(out_ref.shape).astype(out_ref.dtype)


def down_product(acts, downs):
    rows, hidden = acts[0].shape
    width = downs[0].shape[1]
    block = 256
    tall = width // 128
    return pl.pallas_call(
        down_kernel,
        grid=(rows // block,),
        in_specs=[pl.BlockSpec((block, hidden), lambda i: (i, 0))] * 4
        + [pl.BlockSpec((hidden, width), lambda i: (0, 0))] * 4,
        out_specs=pl.BlockSpec((block, tall, 128), lambda i: (i, 0, 0)),
        out_shape=jax.ShapeDtypeStruct((rows, tall, 128), jnp.bfloat16),
        compiler_params=pltpu.CompilerParams(vmem_limit_bytes=VMEM),
        cost_estimate=pl.CostEstimate(
            flops=8 * rows * hidden * width,
            bytes_accessed=2 * (4 * hidden * width + rows * width + 4 * rows * hidden),
            transcendentals=0,
        ),
    )(*acts, *downs)


def shards(tokens, expert_ids, gate_values, pair_order, w_gate, w_up, w_down, sketch):
    rows_dev, width = tokens.shape
    experts = lax.axis_size("expert")
    groups = lax.axis_size("dp")
    lanes = 128
    tall = width // lanes
    ranks = pick_ranks(expert_ids)

    def place_of(first, count):
        inside = (ranks >= first) & (ranks < first + count)
        return jnp.where(inside, expert_ids * count + ranks - first, -1)

    places, first = [], 0
    for count in CHUNKS:
        places.append(place_of(first, count))
        first += count

    place = lax.axis_index("dp")
    columns = width // groups

    def down_columns(by):
        start = lax.rem(place + by, groups) * columns
        return lax.dynamic_slice_in_dim(w_down[0], start, columns, axis=1)

    down_parts = tuple(down_columns(by) for by in (0, 1, groups - 1, 2))
    def outgoing_rows(count, place):
        spots = jnp.arange(experts * count, dtype=jnp.int32)
        select = jnp.any(place[None, :, :] == spots[:, None, None], axis=2)
        placed = jnp.dot(select.astype(jnp.bfloat16), tokens, preferred_element_type=jnp.float32)
        return placed.astype(jnp.bfloat16).reshape(experts, count * tall, lanes)

    def halves(incoming, count):
        middle = experts // 2
        parts = (incoming[:middle], incoming[middle:])
        return tuple(part.reshape(middle * count, width) for part in parts)

    def dispatch(outgoing):
        return lax.all_to_all(outgoing, "expert", split_axis=0, concat_axis=0, tiled=True)

    outgoing = outgoing_rows(CHUNKS[0], places[0])
    downs = tuple(shift(part, by) if by else part for part, by in zip(down_parts, (0, 1, -1, 2)))
    own = halves(dispatch(outgoing), CHUNKS[0])
    next_outgoing = outgoing_rows(CHUNKS[1], places[1])
    next_outgoing, own = lax.optimization_barrier((next_outgoing, own))
    next_outgoing, downs = lax.optimization_barrier((next_outgoing, downs))
    next_arrived = dispatch(next_outgoing)
    first = gather_neighbours(own)
    next_arrived, _, _ = lax.optimization_barrier((next_arrived, first[0], first[3]))
    second = (shift(first[0], 1), shift(first[3], -1))
    late_sketch, next_arrived = lax.optimization_barrier((sketch, next_arrived))
    full_sketch = lax.all_gather(late_sketch, "expert", axis=0, tiled=True)
    next_own = halves(next_arrived, CHUNKS[1])
    next_first = list(gather_neighbours(next_own))
    second, _, _ = lax.optimization_barrier(
        (second, next_first[0], next_first[3])
    )
    next_second = (shift(next_first[0], 1), shift(next_first[3], -1))
    act = hidden_units((*own, *first, *second), w_gate, w_up)
    acts = (act, shift(act, 1), shift(act, -1), shift(act, 2))
    next_second, act = lax.optimization_barrier((next_second, act))
    next_act = hidden_units((*next_own, *next_first, *next_second), w_gate, w_up)
    next_acts = (next_act, shift(next_act, 1), shift(next_act, -1), shift(next_act, 2))
    acts, next_act = lax.optimization_barrier((acts, next_act))
    next_acts = (next_act, *next_acts[1:])
    out = down_product(acts, downs)
    out, _ = lax.optimization_barrier((out, next_acts[1:3]))
    next_acts, _ = lax.optimization_barrier((next_acts, out))
    next_acts, full_sketch = lax.optimization_barrier((next_acts, full_sketch))
    outs = (out, down_product(next_acts, downs))

    mixed_sum = jnp.zeros((groups, rows_dev, columns), jnp.float32)
    back = ()
    for count, place, out in zip(CHUNKS, places, outs):
        out = out.reshape(groups * experts, count * (columns // lanes), lanes)
        out, back = lax.optimization_barrier((out, back))
        back = lax.all_to_all(out, ("dp", "expert"), split_axis=0, concat_axis=0, tiled=True)
        back = back.reshape(groups, experts * count, columns)
        spots = jnp.arange(experts * count, dtype=jnp.int32)
        matches = place[:, :, None] == spots[None, None, :]
        weights = jnp.sum(
            jnp.where(matches, gate_values[:, :, None], jnp.zeros((), jnp.bfloat16)), axis=1
        )
        mixed_sum = mixed_sum + jnp.einsum(
            "ts,gsc->gtc", weights, back, preferred_element_type=jnp.float32
        )
    mixed_parts = mixed_sum.astype(jnp.bfloat16)
    mixed = jnp.transpose(mixed_parts, (1, 0, 2)).reshape(rows_dev, width)

    pairs = rows_dev // 2
    order = pair_order[0].reshape(pairs, 2)
    row_ids = jnp.arange(rows_dev, dtype=jnp.int32)
    signs = (order[:, 0:1] == row_ids[None, :]).astype(jnp.bfloat16) - (
        order[:, 1:2] == row_ids[None, :]
    ).astype(jnp.bfloat16)
    contrast = jnp.einsum("pt,gtc->gpc", signs, mixed_parts, preferred_element_type=jnp.float32)
    contrast = contrast.astype(jnp.bfloat16)
    sent = lax.all_to_all(contrast, "dp", split_axis=0, concat_axis=0, tiled=True)
    projected = jnp.einsum(
        "gpc,gck->pk",
        contrast,
        full_sketch.reshape(groups, columns, -1),
        preferred_element_type=jnp.float32,
    ).astype(jnp.bfloat16)
    nearby = (projected, shift(projected, -1), shift(projected, 2), shift(projected, 1))
    here = lax.axis_index("dp")
    projected = jnp.concatenate(
        [
            lax.select_n(lax.rem(g - here + groups, groups), *nearby)
            for g in range(groups)
        ],
        axis=0,
    )
    covariance = lax.dot_general(
        sent.reshape(groups * pairs, columns),
        projected,
        (((0,), (0,)), ((), ())),
        preferred_element_type=jnp.float32,
    )
    parts = covariance.astype(jnp.bfloat16).reshape(experts, -1, covariance.shape[1])
    parts = lax.all_to_all(parts, "expert", split_axis=0, concat_axis=0, tiled=True)
    reading = jnp.sum(parts.astype(jnp.float32), axis=0)
    reading = reading * (1.0 / math.sqrt(pairs * groups * experts))
    return (mixed, reading)


def solution(mesh):
    return jax.shard_map(
        shards,
        mesh=mesh,
        in_specs=(
            P(("dp", "expert"), None),
            P(("dp", "expert"), None),
            P(("dp", "expert"), None),
            P(("dp", "expert"), None),
            P("expert", None, "dp"),
            P("expert", None, "dp"),
            P("expert", "dp", None),
            P("expert", None),
        ),
        out_specs=(P(("dp", "expert"), None), P(("dp", "expert"), None)),
        check_vma=False,
    )
```
